1024 devices in a mesh: rep: 16 (over x, y_hi), fsdp: 64 (over y_lo, z, core).
Axes of the slice: x: 8, y: 8 (y_hi: 2, y_lo: 4; y = y_hi * 4 + y_lo), z: 8, core: 2. Of those that a mesh axis runs over, the one named last changes fastest.
Arguments:
- tokens: bfloat16 [196608, 4096], P(('rep', 'fsdp')), may hold values from -24 to 24
- cotangent: bfloat16 [196608, 256], P(('rep', 'fsdp')), may hold values from -6 to 6
- weight: float32 [4096, 256], P('fsdp'), may hold values from -0.09375 to 0.09375
- momentum: float32 [16, 4096, 256], P('rep', 'fsdp'), may hold values from -6 to 6
- column_order: int32 [64], replicated, may hold values from 0 to 63, each once
Outputs:
- input_grad: bfloat16 [196608, 4096], P(('rep', 'fsdp'))
- new_momentum: float32 [16, 4096, 256], P('rep', 'fsdp')
- update: float32 [4096, 256], P('fsdp')
- new_weight: float32 [4096, 256], P('fsdp')
The draws below stay inside these ranges and needn't reach their ends.
Inputs may be any that keep to these rules, and one draw needn't show every extreme that they name: `column_order`: each of the 64 frequency indices appears exactly once.
All inputs are finite; a program needn't handle non-finite values.
Results may differ from the reference program's by a relative error of at most 0.0049.
Values may be sent and summed in bfloat16 or wider, within the bound.
A program may use at most 32 MiB of HBM per device.

```python
import math
import jax
import jax.numpy as jnp
from jax import lax

D = 4096
KW = 256
BLOCK = 64
SEL = 16
GROUP_TOK = 12288
ALL_TOK = 196608
N_REP = 16


def strengthened(drawn, own_key, source, target, shards_of, factor):
    owner, partner = [(jnp.arange(drawn.shape[dim]) // (drawn.shape[dim] // shards_of)).reshape([-1 if axis == dim else 1 for axis in range(drawn.ndim)]) for dim in (source, target)]
    chosen = jax.random.permutation(own_key, shards_of)[partner]
    strong = (owner == chosen) | (owner == (partner + shards_of // 2) % shards_of)
    return jnp.where(strong, factor * drawn, drawn)


def block_scale(rng, dims, shards, least, top_value):
    factor_of = 1.0
    for axis_at, parts in shards:
        heights = jax.random.uniform(jax.random.fold_in(jax.random.fold_in(rng, 6), axis_at), (parts,), jnp.float32, least / len(shards), top_value / len(shards))
        factor_of = factor_of * jnp.repeat(jnp.exp(heights), dims[axis_at] // parts).reshape((-1,) + (1,) * (len(dims) - 1 - axis_at))
    return factor_of


def centred(key, shape, deviation, bound, split=(), kind=jnp.bfloat16):
    entries = jax.random.normal(key, shape, jnp.float32) * deviation
    if len(split) > 0:
        entries = block_scale(key, shape, split, -0.22, 0.18) * entries
    return jnp.clip(entries, min=-bound, max=bound).astype(kind)


def noise_with(rng, extent, deviation, limit, cuts, heavy, dtype=jnp.bfloat16):
    result = deviation * jax.random.normal(rng, extent, jnp.float32)
    if cuts:
        result = result * block_scale(rng, extent, cuts, -0.22, 0.18)
    return jnp.clip(strengthened(result, jax.random.fold_in(rng, 3), *heavy), -limit, limit).astype(dtype)


def setup_inputs(seed: int = 0) -> dict:
    key_list = jax.random.split(jax.random.key(seed), 6)
    tokens = noise_with(key_list[0], (ALL_TOK, D), 1.0, 24.0, ((0, 1024),), (0, 1, 1024, 6.0))
    cotangent = centred(key_list[1], (ALL_TOK, KW), 1.0, 6.0, ((0, 1024),))
    weight = centred(key_list[2], (D, KW), D ** -0.5, 0.09375, ((0, 64),), jnp.float32)
    momentum = centred(key_list[3], (N_REP, D, KW), 1.0, 6.0, ((0, 16), (1, 64)), jnp.float32)
    column_order = jax.random.permutation(key_list[4], BLOCK).astype(jnp.int32)
    return {"tokens": tokens, "cotangent": cotangent, "weight": weight, "momentum": momentum, "column_order": column_order}


MOMENTUM_DECAY = 0.9
LEARN_RATE = 0.05

def dct_table():
    index = jnp.arange(BLOCK).astype(jnp.float32)
    table = jnp.cos(math.pi * (2.0 * index[None, :] + 1.0) * index[:, None] / (2.0 * BLOCK)) * math.sqrt(2.0 / BLOCK)
    return jnp.where(index[:, None] == 0.0, table * math.sqrt(0.5), table)

def forward_blocks(field, table):
    rows, cols = field.shape
    blocks = field.reshape(rows // BLOCK, BLOCK, cols // BLOCK, BLOCK)
    out = jnp.einsum('kn,anbm,lm->akbl', table, blocks, table, precision=lax.Precision.HIGHEST)
    return out.reshape(rows, cols)

def inverse_blocks(field, table):
    rows, cols = field.shape
    blocks = field.reshape(rows // BLOCK, BLOCK, cols // BLOCK, BLOCK)
    out = jnp.einsum('kn,akbl,lm->anbm', table, blocks, table, precision=lax.Precision.HIGHEST)
    return out.reshape(rows, cols)

def reference(tokens, cotangent, weight, momentum, column_order):
    table = dct_table()
    weight_half = weight.astype(jnp.bfloat16)
    chosen = jnp.any(jnp.arange(BLOCK).astype(jnp.int32)[:, None] == column_order[None, :SEL], axis=1)
    col_mask = jnp.tile(chosen.astype(jnp.float32), KW // BLOCK)
    tok_groups = tokens.reshape(N_REP, GROUP_TOK, D)
    cot_groups = cotangent.reshape(N_REP, GROUP_TOK, KW)
    scale = float(GROUP_TOK) ** (-0.5)

    def per_replica(items):
        tok_part, cot_part, moment_old = items
        input_part = lax.dot_general(cot_part, weight_half, (((1,), (1,)), ((), ())), preferred_element_type=jnp.float32).astype(jnp.bfloat16)
        weight_grad = lax.dot_general(tok_part, cot_part, (((0,), (0,)), ((), ())), preferred_element_type=jnp.float32) * scale
        moment = MOMENTUM_DECAY * moment_old + weight_grad
        coeffs = forward_blocks(moment, table)
        sent = coeffs * col_mask[None, :]
        return (input_part, moment - inverse_blocks(sent, table), sent)
    input_grad, new_momentum, sent = lax.map(per_replica, (tok_groups, cot_groups, momentum))
    update = inverse_blocks(lax.optimization_barrier(jnp.sum(sent, axis=0)), table) / N_REP
    new_weight = weight - LEARN_RATE * update
    return (input_grad.reshape(ALL_TOK, D), new_momentum, update, new_weight)
```

```python
import math

import jax
import jax.numpy as jnp
import numpy as np
from jax import lax
from jax.experimental import pallas as pl
from jax.experimental.pallas import tpu as pltpu
from jax.sharding import PartitionSpec as P

KW = 256
BLOCK = 64
SEL = 16
NX, NYH, NY, NZ = 8, 2, 4, 8
GROUP_TOK = 12288
MOMENTUM_DECAY = 0.9
LEARN_RATE = 0.05
MESH = pl.DeviceIdType.MESH
F32 = jnp.float32
BF16 = jnp.bfloat16
HI = lax.Precision.HIGHEST

UP = (2, 1)
DOWN = (3, 0)


def dct_rows():
    n = np.arange(BLOCK, dtype=np.float64)
    table = np.cos(math.pi * (2.0 * n[None, :] + 1.0) * n[:, None] / (2.0 * BLOCK)) * math.sqrt(2.0 / BLOCK)
    table[0] *= math.sqrt(0.5)
    return np.tile(table.T, (KW // BLOCK, 1)).astype(np.float32)


def make_slots():
    slots = {}

    def slot(*key):
        if key not in slots:
            slots[key] = len(slots)
        return slots[key]

    return slot


N_SLOTS = 112


def body(
    order, tok, cot, weight, mom, dct,
    ig, nm, up, nw,
    wf, own, psend, precv, rsend, rrecv, ysend, yrecv, c1s, c1r, c2r,
    ss, rs,
):
    slot = make_slots()
    rep = lax.axis_index("rep")
    mem = lax.axis_index("fsdp")
    x, yh = rep // 2, rep % 2
    y, z, core = mem // 16, (mem // 2) % 8, mem % 2

    def dev(x_, yh_, y_, z_, core_):
        return (x_ * 2 + yh_, y_ * 16 + z_ * 2 + core_)

    def at_z(d):
        return dev(x, yh, y, lax.rem(z + d, NZ), core)

    def at_y(e):
        return dev(x, yh, lax.rem(y + e, NY), z, core)

    def at_ring_y(d):
        full = lax.rem(yh * NY + y + d, NY * NYH)
        return dev(x, full // NY, full % NY, z, core)

    def at_x(d):
        return dev(lax.rem(x + d, NX), yh, y, z, core)

    sibling = dev(x, yh, y, z, 1 - core)
    mirror = dev(x, 1 - yh, y, z, core)

    partners = [sibling, mirror]
    partners += [at_z(d) for d in range(1, NZ)]
    partners += [at_x(d) for d in range(1, NX)]
    partners += [at_y(e) for e in range(1, NY)]
    partners += [at_ring_y(d) for d in (1, 2, 6, 7)]
    barrier = pltpu.get_barrier_semaphore()
    for p in partners:
        pl.semaphore_signal(barrier, inc=1, device_id=p, device_id_type=MESH)

    started = []

    def copy(key, src, dst, device):
        i = slot(*key)
        return pltpu.make_async_remote_copy(
            src_ref=src, dst_ref=dst, send_sem=ss.at[i], recv_sem=rs.at[i],
            device_id=device, device_id_type=MESH,
        )

    def send(key, src, dst, device):
        c = copy(key, src, dst, device)
        c.start()
        started.append(c)

    def arrived(key, dst):
        copy(key, dst, dst, sibling).wait_recv()

    chip = y * NZ + z

    def piece(x_):
        return x_ % 2, x_ // 2

    half, rb = piece(x)
    wf[half, chip, core, rb] = weight[
        pl.ds(pl.multiple_of(rb * 16, 16), 16), pl.ds(pl.multiple_of(half * 128, 128), 128)
    ].astype(BF16)

    pl.semaphore_wait(barrier, len(partners))

    own_piece = wf.at[half, chip, core, rb]
    for d in range(1, NZ):
        send(("gz", d), own_piece, own_piece, at_z(d))

    def partial(d):
        for e in range(NY):
            target = lax.rem(y + e, NY) * NZ + lax.rem(z + d, NZ)
            both = lax.dot_general(
                tok[:, pl.ds(pl.multiple_of(target * 128, 128), 128)], cot[...],
                (((0,), (0,)), ((), ())), preferred_element_type=F32,
            )
            low, high = both[:64], both[64:]
            own[d, e] = jnp.where(core == 0, low, high)
            psend[d, e] = jnp.where(core == 0, high, low).astype(BF16)
        send(("pair", d), psend.at[d], precv.at[d], sibling)

    for d in (4, 3, 5, 2, 6, 1, 7, 0):
        partial(d)

    def hop(h, direction, e):
        d = 4 - h if direction == 0 else 4 + h
        total = own[d, e] + precv[d, e].astype(F32)
        first = UP if direction == 0 else DOWN
        if h > 1 or (h == 1 and e in first):
            arrived(("ring", direction, h - 1, e), rrecv.at[direction, h - 1, e])
            total = total + rrecv[direction, h - 1, e].astype(F32)
        rsend[direction, h, e] = total.astype(BF16)
        send(
            ("ring", direction, h, e), rsend.at[direction, h, e], rrecv.at[direction, h, e],
            at_z(1 if direction == 0 else 7),
        )

    arrived(("pair", 4), precv.at[4])
    for i in range(2):
        hop(0, 0, UP[i])
        hop(0, 1, DOWN[i])
    arrived(("pair", 3), precv.at[3])
    arrived(("pair", 5), precv.at[5])
    for i in range(2):
        hop(1, 0, DOWN[i])
        hop(1, 1, UP[i])

    for d in range(1, NZ):
        arrived(("gz", d), own_piece)
    y_block = wf.at[half, pl.ds(y * NZ, NZ), core, rb]
    for d in (1, 7, 2):
        send(("gy", d), y_block, y_block, at_ring_y(d))

    for i in range(2):
        hop(1, 0, UP[i])
        hop(1, 1, DOWN[i])

    for d in (1, 7, 2):
        arrived(("gy", d), y_block)

    def x_part(x_, part):
        h_, r_ = piece(x_)
        return wf.at[h_, pl.ds(part * 16, 16), core, r_]

    def x_all(x_):
        h_, r_ = piece(x_)
        return wf.at[h_, :, core, r_]

    def gather_x(h, direction):
        origin = lax.rem(x + (NX - h if direction == 0 else h), NX)
        parts = (0, 1) if h < 3 else (direction,)
        for part in (0, 1):
            ref = x_part(origin, part)
            if h > 0:
                arrived(("gx", direction, h - 1, part), ref)
            if part in parts:
                send(("gx", direction, h, part), ref, ref, at_x(1 if direction == 0 else 7))
        if h > 0:
            send(("gc", direction, h), x_all(origin), x_all(origin), sibling)

    for direction in (0, 1):
        gather_x(0, direction)
    send(("gc", 0, 0), x_all(x), x_all(x), sibling)

    arrived(("pair", 2), precv.at[2])
    arrived(("pair", 6), precv.at[6])
    for i in range(2):
        hop(2, 0, DOWN[i])
        hop(2, 1, UP[i])
    for i in range(2):
        hop(2, 0, UP[i])
        hop(2, 1, DOWN[i])

    row = lax.broadcasted_iota(jnp.int32, (BLOCK, 128), 0)
    lane = lax.broadcasted_iota(jnp.int32, (BLOCK, 128), 1)
    picked = jnp.zeros((BLOCK, 128), F32)
    for s in range(SEL):
        picked = jnp.where((lane % SEL == s) & (row == order[s]), 1.0, picked)
    wide = lax.dot_general(dct[...], picked, (((1,), (0,)), ((), ())), precision=HI, preferred_element_type=F32)
    row_block = lax.broadcasted_iota(jnp.int32, (KW, 128), 0) // BLOCK
    lane_block = lax.broadcasted_iota(jnp.int32, (KW, 128), 1) // SEL
    basis0 = jnp.where(row_block == lane_block, wide, 0.0)
    basis1 = jnp.where(row_block + 4 == lane_block, wide, 0.0)

    gather_x(1, 0)
    gather_x(1, 1)

    arrived(("pair", 1), precv.at[1])
    arrived(("pair", 7), precv.at[7])
    for i in range(2):
        hop(3, 0, DOWN[i])
        hop(3, 1, UP[i])
    for i in range(2):
        hop(3, 0, UP[i])
        hop(3, 1, DOWN[i])

    gather_x(2, 0)
    gather_x(2, 1)

    arrived(("pair", 0), precv.at[0])

    def z_total(e):
        total = own[0, e] + precv[0, e].astype(F32)
        for direction in (0, 1):
            arrived(("ring", direction, 3, e), rrecv.at[direction, 3, e])
            total = total + rrecv[direction, 3, e].astype(F32)
        return total

    for e in (2, 3, 1):
        ysend[e] = z_total(e).astype(BF16)
        send(("y", e), ysend.at[e], yrecv.at[e], at_y(e))
    grad = z_total(0)

    gather_x(3, 0)
    gather_x(3, 1)

    for e in (1, 3, 2):
        arrived(("y", e), yrecv.at[e])
        grad = grad + yrecv[e].astype(F32)

    moment = MOMENTUM_DECAY * mom[0] + grad * (float(GROUP_TOK) ** -0.5)
    compact = lax.dot_general(
        moment[:32], basis0, (((1,), (0,)), ((), ())), precision=HI, preferred_element_type=F32
    ) + lax.dot_general(
        moment[32:], basis1, (((1,), (0,)), ((), ())), precision=HI, preferred_element_type=F32
    )
    c1s[...] = compact
    send(("mirror",), c1s, c1r, mirror)

    nm[0, :32] = moment[:32] - lax.dot_general(
        compact, basis0, (((1,), (1,)), ((), ())), precision=HI, preferred_element_type=F32
    )
    nm[0, 32:] = moment[32:] - lax.dot_general(
        compact, basis1, (((1,), (1,)), ((), ())), precision=HI, preferred_element_type=F32
    )

    arrived(("mirror",), c1r)
    c2r[x] = (compact + c1r[...]).astype(BF16)
    for d in range(1, NX):
        send(("rep", d), c2r.at[x], c2r.at[x], at_x(d))

    far = lax.rem(x + 4, NX)
    arrived(("gx", 0, 3, 0), x_part(far, 0))
    arrived(("gx", 1, 3, 1), x_part(far, 1))
    send(("gc", 0, 4), x_all(far), x_all(far), sibling)
    for key in [("gc", 0, h) for h in range(5)] + [("gc", 1, h) for h in range(1, 4)]:
        arrived(key, x_all(x))

    for i in range(8):
        w = jnp.concatenate(
            [wf[k, 4 * i:4 * i + 4].reshape(512, 128) for k in range(2)], axis=1
        )
        ig[:, 512 * i:512 * i + 512] = lax.dot_general(
            cot[...], w, (((1,), (1,)), ((), ())), preferred_element_type=F32
        ).astype(BF16)

    for d in range(1, NX):
        arrived(("rep", d), c2r.at[0])
    total = c2r[0].astype(F32)
    for i in range(1, NX):
        total = total + c2r[i].astype(F32)
    total = total * (1.0 / (NX * NYH))
    for i, basis in enumerate((basis0, basis1)):
        rows = slice(32 * i, 32 * i + 32)
        update = lax.dot_general(total, basis, (((1,), (1,)), ((), ())), precision=HI, preferred_element_type=F32)
        up[rows] = update
        nw[rows] = weight[rows] - LEARN_RATE * update

    for c in started:
        c.wait_send()


def on_device(tokens, cotangent, weight, momentum, column_order):
    vmem = pl.BlockSpec(memory_space=pltpu.VMEM)
    smem = pl.BlockSpec(memory_space=pltpu.SMEM)
    return pl.pallas_call(
        body,
        out_shape=(
            jax.ShapeDtypeStruct((tokens.shape[0], tokens.shape[1]), BF16),
            jax.ShapeDtypeStruct(momentum.shape, F32),
            jax.ShapeDtypeStruct(weight.shape, F32),
            jax.ShapeDtypeStruct(weight.shape, F32),
        ),
        in_specs=[smem, vmem, vmem, vmem, vmem, vmem],
        out_specs=(vmem, vmem, vmem, vmem),
        scratch_shapes=[
            pltpu.VMEM((2, NY * NZ, 2, 4, 16, 128), BF16),
            pltpu.VMEM((NZ, NY, 64, KW), F32),
            pltpu.VMEM((NZ, NY, 64, KW), BF16),
            pltpu.VMEM((NZ, NY, 64, KW), BF16),
            pltpu.VMEM((2, 4, NY, 64, KW), BF16),
            pltpu.VMEM((2, 4, NY, 64, KW), BF16),
            pltpu.VMEM((NY, 64, KW), BF16),
            pltpu.VMEM((NY, 64, KW), BF16),
            pltpu.VMEM((32, 128), F32),
            pltpu.VMEM((32, 128), F32),
            pltpu.VMEM((NX, 32, 128), BF16),
            pltpu.SemaphoreType.DMA((N_SLOTS,)),
            pltpu.SemaphoreType.DMA((N_SLOTS,)),
        ],
        compiler_params=pltpu.CompilerParams(
            collective_id=0, has_side_effects=True, vmem_limit_bytes=40 * 1024 * 1024
        ),
        name="demo_step",
    )(column_order, tokens, cotangent, weight, momentum, jnp.asarray(dct_rows()))


def solution(mesh):
    in_specs = (
        P(("rep", "fsdp"), None),
        P(("rep", "fsdp"), None),
        P("fsdp", None),
        P("rep", "fsdp", None),
        P(),
    )
    out_specs = (P(("rep", "fsdp"), None), P("rep", "fsdp", None), P("fsdp", None), P("fsdp", None))
    return jax.shard_map(
        on_device, mesh=mesh, in_specs=in_specs, out_specs=out_specs, check_vma=False
    )
```

```python
import math

import jax
import jax.numpy as jnp
import numpy as np
from jax import lax
from jax.experimental import pallas as pl
from jax.experimental.pallas import tpu as pltpu
from jax.sharding import PartitionSpec as P

KW = 256
BLOCK = 64
SEL = 16
NX, NYH, NY, NZ = 8, 2, 4, 8
GROUP_TOK = 12288
MOMENTUM_DECAY = 0.9
LEARN_RATE = 0.05
MESH = pl.DeviceIdType.MESH
F32 = jnp.float32
BF16 = jnp.bfloat16
HI = lax.Precision.HIGHEST

UP = (2, 1)
DOWN = (3, 0)
LATE = (2, 3, 1, 0)

PARTS = (0, 1, 3, 2)
LAST = ((0, 3), (1, 2))


def dct_rows():
    n = np.arange(BLOCK, dtype=np.float64)
    table = np.cos(math.pi * (2.0 * n[None, :] + 1.0) * n[:, None] / (2.0 * BLOCK)) * math.sqrt(2.0 / BLOCK)
    table[0] *= math.sqrt(0.5)
    return np.tile(table.T, (KW // BLOCK, 1)).astype(np.float32)


def make_slots():
    slots = {}

    def slot(*key):
        if key not in slots:
            slots[key] = len(slots)
        return slots[key]

    return slot


N_SLOTS = 128


def body(
    order_hbm, tok_hbm, cot_hbm, weight_hbm, mom_hbm, dct_hbm,
    ig_hbm, nm_hbm, up_hbm, nw_hbm,
    ig, nm, up, nw,
    order, tok, cot, weight, mom, dct,
    wf, own, psend, precv, rsend, rrecv, ysend, yrecv, csend, crecv, cmom, c2r,
    ss, rs, ls,
):
    slot = make_slots()
    local = [
        pltpu.make_async_copy(src, dst, ls.at[i])
        for i, (src, dst) in enumerate((
            (weight_hbm, weight), (cot_hbm, cot), (tok_hbm, tok), (mom_hbm, mom), (dct_hbm, dct), (order_hbm, order),
        ))
    ]
    for c in local:
        c.start()
    rep = lax.axis_index("rep")
    mem = lax.axis_index("fsdp")
    x, yh = rep // 2, rep % 2
    y, z, core = mem // 16, (mem // 2) % 8, mem % 2

    def dev(x_, yh_, y_, z_, core_):
        return (x_ * 2 + yh_, y_ * 16 + z_ * 2 + core_)

    def at_z(d):
        return dev(x, yh, y, lax.rem(z + d, NZ), core)

    def at_y(e):
        return dev(x, yh, lax.rem(y + e, NY), z, core)

    def across(e):
        return dev(x, 1 - yh, lax.rem(y + e, NY), z, core)

    def at_ring_y(d):
        full = lax.rem(yh * NY + y + d, NY * NYH)
        return dev(x, full // NY, full % NY, z, core)

    def at_x(d):
        return dev(lax.rem(x + d, NX), yh, y, z, core)

    sibling = dev(x, yh, y, z, 1 - core)

    partners = [sibling, across(0)]
    partners += [at_z(d) for d in range(1, NZ)]
    partners += [at_x(d) for d in range(1, NX)]
    partners += [at_y(e) for e in range(1, NY)]
    partners += [at_ring_y(d) for d in (1, 2, 6, 7)]
    partners += [across(e) for e in range(1, NY)]
    barrier = pltpu.get_barrier_semaphore()
    for p in partners:
        pl.semaphore_signal(barrier, inc=1, device_id=p, device_id_type=MESH)

    started = []
    stores = []

    def store(i, src, dst):
        c = pltpu.make_async_copy(src, dst, ls.at[i])
        c.start()
        stores.append(c)

    def copy(key, src, dst, device):
        i = slot(*key)
        return pltpu.make_async_remote_copy(
            src_ref=src, dst_ref=dst, send_sem=ss.at[i], recv_sem=rs.at[i],
            device_id=device, device_id_type=MESH,
        )

    def send(key, src, dst, device):
        c = copy(key, src, dst, device)
        c.start()
        started.append(c)

    def arrived(key, dst):
        copy(key, dst, dst, sibling).wait_recv()

    def partial(d):
        for e in range(NY):
            target = lax.rem(y + e, NY) * NZ + lax.rem(z + d, NZ)
            both = lax.dot_general(
                tok[:, pl.ds(pl.multiple_of(target * 128, 128), 128)], cot[...],
                (((0,), (0,)), ((), ())), preferred_element_type=F32,
            )
            low, high = both[:64], both[64:]
            own[d, e] = jnp.where(core == 0, low, high)
            psend[d, e] = jnp.where(core == 0, high, low).astype(BF16)

    def pair(d):
        send(("pair", d), psend.at[d], precv.at[d], sibling)

    chip = y * NZ + z

    def piece(x_):
        return x_ % 2, x_ // 2

    half, rb = piece(x)
    local[0].wait()
    wf[half, chip, core, rb] = weight[
        pl.ds(pl.multiple_of(rb * 16, 16), 16), pl.ds(pl.multiple_of(half * 128, 128), 128)
    ].astype(BF16)
    own_piece = wf.at[half, chip, core, rb]

    local[1].wait()
    local[2].wait()
    for d in (4, 3, 5):
        partial(d)

    pl.semaphore_wait(barrier, len(partners))

    for d in (4, 3, 5):
        pair(d)
    for d in range(1, NZ):
        send(("gz", d), own_piece, own_piece, at_z(d))

    def hop(h, direction, e):
        d = 4 - h if direction == 0 else 4 + h
        total = own[d, e] + precv[d, e].astype(F32)
        first = UP if direction == 0 else DOWN
        if h > 1 or (h == 1 and e in first):
            arrived(("ring", direction, h - 1, e), rrecv.at[direction, h - 1, e])
            total = total + rrecv[direction, h - 1, e].astype(F32)
        rsend[direction, h, e] = total.astype(BF16)
        send(
            ("ring", direction, h, e), rsend.at[direction, h, e], rrecv.at[direction, h, e],
            at_z(1 if direction == 0 else 7),
        )

    def x_part(x_, e):
        h_, r_ = piece(x_)
        return wf.at[h_, pl.ds(lax.rem(y + e, NY) * NZ, NZ), core, r_]

    def x_all(x_):
        h_, r_ = piece(x_)
        return wf.at[h_, :, core, r_]

    def origin(h, direction):
        return lax.rem(x + (NX - h if direction == 0 else h), NX)

    def gather_x(h, direction, e):
        ref = x_part(origin(h, direction), e)
        if h > 0:
            arrived(("gx", direction, h - 1, e), ref)
        if h < 3 or e in LAST[direction]:
            send(("gx", direction, h, e), ref, ref, at_x(1 if direction == 0 else 7))

    def gather_core(h, direction):
        ref = x_all(origin(h, direction))
        send(("gc", direction, h), ref, ref, sibling)

    for d in (2, 6):
        partial(d)
        pair(d)
    arrived(("pair", 4), precv.at[4])
    for i in range(2):
        hop(0, 0, UP[i])
        hop(0, 1, DOWN[i])
    for d in (1, 7, 0):
        partial(d)
        pair(d)
    arrived(("pair", 3), precv.at[3])
    arrived(("pair", 5), precv.at[5])
    for i in range(2):
        hop(1, 0, DOWN[i])
        hop(1, 1, UP[i])

    for i in range(2):
        hop(1, 0, UP[i])
        hop(1, 1, DOWN[i])

    for d in range(1, NZ):
        arrived(("gz", d), own_piece)
    y_block = x_part(x, 0)
    for d in (1, 7, 2):
        send(("gy", d), y_block, y_block, at_ring_y(d))
    for direction in (0, 1):
        gather_x(0, direction, 0)

    for i in (3, 4, 5):
        local[i].wait()

    row = lax.broadcasted_iota(jnp.int32, (BLOCK, 128), 0)
    lane = lax.broadcasted_iota(jnp.int32, (BLOCK, 128), 1)
    picked = jnp.zeros((BLOCK, 128), F32)
    for s in range(SEL):
        picked = jnp.where((lane % SEL == s) & (row == order[s]), 1.0, picked)
    wide = lax.dot_general(dct[...], picked, (((1,), (0,)), ((), ())), precision=HI, preferred_element_type=F32)
    row_block = lax.broadcasted_iota(jnp.int32, (KW, 128), 0) // BLOCK
    lane_block = lax.broadcasted_iota(jnp.int32, (KW, 128), 1) // SEL
    basis0 = jnp.where(row_block == lane_block, wide, 0.0)
    basis1 = jnp.where(row_block + 4 == lane_block, wide, 0.0)

    def project(upper, lower):
        return lax.dot_general(
            upper, basis0, (((1,), (0,)), ((), ())), precision=HI, preferred_element_type=F32
        ) + lax.dot_general(
            lower, basis1, (((1,), (0,)), ((), ())), precision=HI, preferred_element_type=F32
        )

    decayed = MOMENTUM_DECAY * mom[0]
    cmom[yh] = project(decayed[:32], decayed[32:])
    send(("old",), cmom.at[yh], cmom.at[yh], across(0))

    arrived(("pair", 2), precv.at[2])
    arrived(("pair", 6), precv.at[6])
    for e in LATE:
        hop(2, 0, e)
        hop(2, 1, e)

    for d, e in ((7, 1), (1, 3), (2, 2)):
        arrived(("gy", d), x_part(x, e))
        for direction in (0, 1):
            gather_x(0, direction, e)
    gather_core(0, 0)

    arrived(("pair", 1), precv.at[1])
    arrived(("pair", 7), precv.at[7])
    for e in LATE:
        hop(3, 0, e)
        hop(3, 1, e)

    def gather_step(h):
        for e in PARTS:
            gather_x(h, 0, e)
            gather_x(h, 1, e)
        gather_core(h, 0)
        gather_core(h, 1)

    gather_step(1)

    arrived(("pair", 0), precv.at[0])

    def z_total(e):
        total = own[0, e] + precv[0, e].astype(F32)
        for direction in (0, 1):
            arrived(("ring", direction, 3, e), rrecv.at[direction, 3, e])
            total = total + rrecv[direction, 3, e].astype(F32)
        return total

    place = yh * NY + y
    for both in (LATE[:2], LATE[2:]):
        sums = [z_total(e) for e in both]
        columns = project(
            jnp.concatenate([t[:32] for t in sums], axis=0), jnp.concatenate([t[32:] for t in sums], axis=0)
        ).astype(BF16)
        for i, e in enumerate(both):
            csend[e] = columns[32 * i:32 * i + 32]
            send(("across", e), csend.at[e], crecv.at[place], across(e))
            if e > 0:
                send(("along", e), csend.at[e], crecv.at[place], at_y(e))
            else:
                crecv[place] = columns[32 * i:32 * i + 32]
        for i, e in enumerate(both):
            if e > 0:
                ysend[e] = sums[i].astype(BF16)
                send(("y", e), ysend.at[e], yrecv.at[e], at_y(e))
            else:
                grad = sums[i]

    gather_step(2)

    scale = float(GROUP_TOK) ** -0.5
    arrived(("old",), cmom.at[0])
    for e in LATE[:3]:
        arrived(("along", e), crecv.at[0])
    for e in LATE:
        arrived(("across", e), crecv.at[0])
    shared = crecv[0].astype(F32)
    for i in range(1, NYH * NY):
        shared = shared + crecv[i].astype(F32)
    c2r[x] = (shared * scale + (cmom[0] + cmom[1])).astype(BF16)
    for d in (4, 3, 5, 2, 6, 1, 7):
        send(("rep", d), c2r.at[x], c2r.at[x], at_x(d))

    gather_step(3)

    for e in LATE[:3]:
        arrived(("y", e), yrecv.at[e])
        grad = grad + yrecv[e].astype(F32)
    moment = decayed + grad * scale
    compact = project(moment[:32], moment[32:])
    nm[0, :32] = moment[:32] - lax.dot_general(
        compact, basis0, (((1,), (1,)), ((), ())), precision=HI, preferred_element_type=F32
    )
    nm[0, 32:] = moment[32:] - lax.dot_general(
        compact, basis1, (((1,), (1,)), ((), ())), precision=HI, preferred_element_type=F32
    )
    store(6, nm, nm_hbm)

    far = lax.rem(x + 4, NX)
    for direction in (0, 1):
        for e in LAST[direction]:
            arrived(("gx", direction, 3, e), x_part(far, e))
    send(("gc", 0, 4), x_all(far), x_all(far), sibling)
    for key in [("gc", 0, h) for h in range(5)] + [("gc", 1, h) for h in range(1, 4)]:
        arrived(key, x_all(x))

    for i in range(8):
        w = jnp.concatenate(
            [wf[k, 4 * i:4 * i + 4].reshape(512, 128) for k in range(2)], axis=1
        )
        ig[:, 512 * i:512 * i + 512] = lax.dot_general(
            cot[...], w, (((1,), (1,)), ((), ())), preferred_element_type=F32
        ).astype(BF16)
    store(7, ig, ig_hbm)

    for d in range(1, NX):
        arrived(("rep", d), c2r.at[0])
    total = c2r[0].astype(F32)
    for i in range(1, NX):
        total = total + c2r[i].astype(F32)
    total = total * (1.0 / (NX * NYH))
    for i, basis in enumerate((basis0, basis1)):
        rows = slice(32 * i, 32 * i + 32)
        update = lax.dot_general(total, basis, (((1,), (1,)), ((), ())), precision=HI, preferred_element_type=F32)
        up[rows] = update
        nw[rows] = weight[rows] - LEARN_RATE * update

    store(8, up, up_hbm)
    store(9, nw, nw_hbm)
    for c in started:
        c.wait_send()
    for c in stores:
        c.wait()


def finish(ig, nm, up, nw, ig_out, nm_out, up_out, nw_out, ig_v, nm_v, up_v, nw_v, sems):
    moves = [(nm, nm_v, nm_out), (up, up_v, up_out), (nw, nw_v, nw_out)]
    rows = ig.shape[0] // 4
    moves += [tuple(r.at[rows * i:rows * i + rows] for r in (ig, ig_v, ig_out)) for i in range(4)]
    loads = [pltpu.make_async_copy(src, mid, sems.at[0, i]) for i, (src, mid, _) in enumerate(moves)]
    stores = [pltpu.make_async_copy(mid, dst, sems.at[1, i]) for i, (_, mid, dst) in enumerate(moves)]
    for c in loads:
        c.start()
    for load, store in zip(loads, stores):
        load.wait()
        store.start()
    for c in stores:
        c.wait()


def on_device(tokens, cotangent, weight, momentum, column_order):
    hbm = pl.BlockSpec(memory_space=pltpu.HBM)
    shapes = (
        jax.ShapeDtypeStruct(tokens.shape, BF16),
        jax.ShapeDtypeStruct(momentum.shape, F32),
        jax.ShapeDtypeStruct(weight.shape, F32),
        jax.ShapeDtypeStruct(weight.shape, F32),
    )
    table = jnp.asarray(dct_rows())
    results = pl.pallas_call(
        body,
        out_shape=shapes,
        in_specs=[hbm] * 6,
        out_specs=(hbm,) * 4,
        scratch_shapes=[pltpu.VMEM(a.shape, a.dtype) for a in shapes] + [
            pltpu.SMEM(column_order.shape, jnp.int32),
            pltpu.VMEM(tokens.shape, BF16),
            pltpu.VMEM(cotangent.shape, BF16),
            pltpu.VMEM(weight.shape, F32),
            pltpu.VMEM(momentum.shape, F32),
            pltpu.VMEM(table.shape, F32),
            pltpu.VMEM((2, NY * NZ, 2, 4, 16, 128), BF16),
            pltpu.VMEM((NZ, NY, 64, KW), F32),
            pltpu.VMEM((NZ, NY, 64, KW), BF16),
            pltpu.VMEM((NZ, NY, 64, KW), BF16),
            pltpu.VMEM((2, 4, NY, 64, KW), BF16),
            pltpu.VMEM((2, 4, NY, 64, KW), BF16),
            pltpu.VMEM((NY, 64, KW), BF16),
            pltpu.VMEM((NY, 64, KW), BF16),
            pltpu.VMEM((NY, 32, 128), BF16),
            pltpu.VMEM((NYH * NY, 32, 128), BF16),
            pltpu.VMEM((NYH, 32, 128), F32),
            pltpu.VMEM((NX, 32, 128), BF16),
            pltpu.SemaphoreType.DMA((N_SLOTS,)),
            pltpu.SemaphoreType.DMA((N_SLOTS,)),
            pltpu.SemaphoreType.DMA((10,)),
        ],
        compiler_params=pltpu.CompilerParams(
            collective_id=0, has_side_effects=True, vmem_limit_bytes=57 * 1024 * 1024
        ),
        name="demo_step",
    )(column_order, tokens, cotangent, weight, momentum, table)
    return pl.pallas_call(
        finish,
        out_shape=shapes,
        in_specs=[hbm] * 4,
        out_specs=(hbm,) * 4,
        scratch_shapes=[pltpu.VMEM(a.shape, a.dtype) for a in shapes] + [pltpu.SemaphoreType.DMA((2, 7))],
        compiler_params=pltpu.CompilerParams(vmem_limit_bytes=57 * 1024 * 1024),
        name="store_results",
    )(*results)


def solution(mesh):
    in_specs = (
        P(("rep", "fsdp"), None),
        P(("rep", "fsdp"), None),
        P("fsdp", None),
        P("rep", "fsdp", None),
        P(),
    )
    out_specs = (P(("rep", "fsdp"), None), P("rep", "fsdp", None), P("fsdp", None), P("fsdp", None))
    return jax.shard_map(
        on_device, mesh=mesh, in_specs=in_specs, out_specs=out_specs, check_vma=False
    )
```

```python
import math

import jax
import jax.numpy as jnp
import numpy as np
from jax import lax
from jax.experimental import pallas as pl
from jax.experimental.pallas import tpu as pltpu
from jax.sharding import PartitionSpec as P

KW = 256
BLOCK = 64
SEL = 16
NX, NYH, NY, NZ = 8, 2, 4, 8
GROUP_TOK = 12288
MOMENTUM_DECAY = 0.9
LEARN_RATE = 0.05
MESH = pl.DeviceIdType.MESH
F32 = jnp.float32
BF16 = jnp.bfloat16
HI = lax.Precision.HIGHEST

UP = (2, 1)
DOWN = (3, 0)
LATE = (2, 3, 1, 0)

PARTS = (0, 1, 3, 2)
LAST = ((0, 3), (1, 2))


def dct_rows():
    n = np.arange(BLOCK, dtype=np.float64)
    table = np.cos(math.pi * (2.0 * n[None, :] + 1.0) * n[:, None] / (2.0 * BLOCK)) * math.sqrt(2.0 / BLOCK)
    table[0] *= math.sqrt(0.5)
    return np.tile(table.T, (KW // BLOCK, 1)).astype(np.float32)


def make_slots():
    slots = {}

    def slot(*key):
        if key not in slots:
            slots[key] = len(slots)
        return slots[key]

    return slot


N_SLOTS = 128


def body(
    order_hbm, tok_hbm, cot_hbm, weight_hbm, mom_hbm, dct_hbm,
    ig_hbm, nm_hbm, up_hbm, nw_hbm,
    ig, nm, up, nw,
    order, tok, cot, weight, mom, dct,
    wf, own, psend, precv, rsend, rrecv, ysend, yrecv, csend, crecv, cmom, c2r,
    ss, rs, ls,
):
    slot = make_slots()
    local = [
        pltpu.make_async_copy(src, dst, ls.at[i])
        for i, (src, dst) in enumerate((
            (weight_hbm, weight), (cot_hbm, cot), (tok_hbm, tok), (mom_hbm, mom), (dct_hbm, dct), (order_hbm, order),
        ))
    ]
    for c in local:
        c.start()
    rep = lax.axis_index("rep")
    mem = lax.axis_index("fsdp")
    x, yh = rep // 2, rep % 2
    y, z, core = mem // 16, (mem // 2) % 8, mem % 2

    def dev(x_, yh_, y_, z_, core_):
        return (x_ * 2 + yh_, y_ * 16 + z_ * 2 + core_)

    def at_z(d):
        return dev(x, yh, y, lax.rem(z + d, NZ), core)

    def at_y(e):
        return dev(x, yh, lax.rem(y + e, NY), z, core)

    def across(e):
        return dev(x, 1 - yh, lax.rem(y + e, NY), z, core)

    def at_ring_y(d):
        full = lax.rem(yh * NY + y + d, NY * NYH)
        return dev(x, full // NY, full % NY, z, core)

    def at_x(d):
        return dev(lax.rem(x + d, NX), yh, y, z, core)

    sibling = dev(x, yh, y, z, 1 - core)

    partners = [sibling, across(0)]
    partners += [at_z(d) for d in range(1, NZ)]
    partners += [at_x(d) for d in range(1, NX)]
    partners += [at_y(e) for e in range(1, NY)]
    partners += [at_ring_y(d) for d in (1, 2, 6, 7)]
    partners += [across(e) for e in range(1, NY)]
    barrier = pltpu.get_barrier_semaphore()
    for p in partners:
        pl.semaphore_signal(barrier, inc=1, device_id=p, device_id_type=MESH)

    started = []
    stores = []

    def store(i, src, dst):
        c = pltpu.make_async_copy(src, dst, ls.at[i])
        c.start()
        stores.append(c)

    def copy(key, src, dst, device):
        i = slot(*key)
        return pltpu.make_async_remote_copy(
            src_ref=src, dst_ref=dst, send_sem=ss.at[i], recv_sem=rs.at[i],
            device_id=device, device_id_type=MESH,
        )

    def send(key, src, dst, device):
        c = copy(key, src, dst, device)
        c.start()
        started.append(c)

    def arrived(key, dst):
        copy(key, dst, dst, sibling).wait_recv()

    def partial(d):
        for e in range(NY):
            target = lax.rem(y + e, NY) * NZ + lax.rem(z + d, NZ)
            both = lax.dot_general(
                tok[:, pl.ds(pl.multiple_of(target * 128, 128), 128)], cot[...],
                (((0,), (0,)), ((), ())), preferred_element_type=F32,
            )
            low, high = both[:64], both[64:]
            own[d, e] = jnp.where(core == 0, low, high)
            psend[d, e] = jnp.where(core == 0, high, low).astype(BF16)

    def pair(d):
        send(("pair", d), psend.at[d], precv.at[d], sibling)

    chip = y * NZ + z

    def piece(x_):
        return x_ % 2, x_ // 2

    half, rb = piece(x)
    local[0].wait()
    wf[half, chip, core, rb] = weight[
        pl.ds(pl.multiple_of(rb * 16, 16), 16), pl.ds(pl.multiple_of(half * 128, 128), 128)
    ].astype(BF16)
    own_piece = wf.at[half, chip, core, rb]

    pl.semaphore_wait(barrier, len(partners))

    for d in (4, 3, 5, 2, 6, 1, 7):
        send(("gz", d), own_piece, own_piece, at_z(d))

    local[1].wait()
    local[2].wait()
    for d in (4, 3, 5):
        partial(d)
        pair(d)

    def hop(h, direction, e):
        d = 4 - h if direction == 0 else 4 + h
        total = own[d, e] + precv[d, e].astype(F32)
        first = UP if direction == 0 else DOWN
        if h > 1 or (h == 1 and e in first):
            arrived(("ring", direction, h - 1, e), rrecv.at[direction, h - 1, e])
            total = total + rrecv[direction, h - 1, e].astype(F32)
        rsend[direction, h, e] = total.astype(BF16)
        send(
            ("ring", direction, h, e), rsend.at[direction, h, e], rrecv.at[direction, h, e],
            at_z(1 if direction == 0 else 7),
        )

    def x_part(x_, e):
        h_, r_ = piece(x_)
        return wf.at[h_, pl.ds(lax.rem(y + e, NY) * NZ, NZ), core, r_]

    def x_all(x_):
        h_, r_ = piece(x_)
        return wf.at[h_, :, core, r_]

    def origin(h, direction):
        return lax.rem(x + (NX - h if direction == 0 else h), NX)

    def gather_x(h, direction, e):
        ref = x_part(origin(h, direction), e)
        if h > 0:
            arrived(("gx", direction, h - 1, e), ref)
        if h < 3 or e in LAST[direction]:
            send(("gx", direction, h, e), ref, ref, at_x(1 if direction == 0 else 7))

    def gather_core(h, direction):
        ref = x_all(origin(h, direction))
        send(("gc", direction, h), ref, ref, sibling)

    for d in (2, 6):
        partial(d)
        pair(d)
    arrived(("pair", 4), precv.at[4])
    for i in range(2):
        hop(0, 0, UP[i])
        hop(0, 1, DOWN[i])
    for d in (1, 7, 0):
        partial(d)
        pair(d)
    arrived(("pair", 3), precv.at[3])
    arrived(("pair", 5), precv.at[5])
    for i in range(2):
        hop(1, 0, DOWN[i])
        hop(1, 1, UP[i])

    for i in range(2):
        hop(1, 0, UP[i])
        hop(1, 1, DOWN[i])

    for d in range(1, NZ):
        arrived(("gz", d), own_piece)
    y_block = x_part(x, 0)
    for d in (1, 7, 2):
        send(("gy", d), y_block, y_block, at_ring_y(d))
    for direction in (0, 1):
        gather_x(0, direction, 0)

    for i in (3, 4, 5):
        local[i].wait()

    row = lax.broadcasted_iota(jnp.int32, (BLOCK, 128), 0)
    lane = lax.broadcasted_iota(jnp.int32, (BLOCK, 128), 1)
    picked = jnp.zeros((BLOCK, 128), F32)
    for s in range(SEL):
        picked = jnp.where((lane % SEL == s) & (row == order[s]), 1.0, picked)
    wide = lax.dot_general(dct[...], picked, (((1,), (0,)), ((), ())), precision=HI, preferred_element_type=F32)
    row_block = lax.broadcasted_iota(jnp.int32, (KW, 128), 0) // BLOCK
    lane_block = lax.broadcasted_iota(jnp.int32, (KW, 128), 1) // SEL
    basis0 = jnp.where(row_block == lane_block, wide, 0.0)
    basis1 = jnp.where(row_block + 4 == lane_block, wide, 0.0)

    def project(upper, lower):
        return lax.dot_general(
            upper, basis0, (((1,), (0,)), ((), ())), precision=HI, preferred_element_type=F32
        ) + lax.dot_general(
            lower, basis1, (((1,), (0,)), ((), ())), precision=HI, preferred_element_type=F32
        )

    decayed = MOMENTUM_DECAY * mom[0]
    cmom[yh] = project(decayed[:32], decayed[32:])
    send(("old",), cmom.at[yh], cmom.at[yh], across(0))

    arrived(("pair", 2), precv.at[2])
    arrived(("pair", 6), precv.at[6])
    for up_e, down_e in zip(DOWN + UP, UP + DOWN):
        hop(2, 0, up_e)
        hop(2, 1, down_e)

    for d, e in ((7, 1), (1, 3), (2, 2)):
        arrived(("gy", d), x_part(x, e))
        for direction in (0, 1):
            gather_x(0, direction, e)
    gather_core(0, 0)

    arrived(("pair", 1), precv.at[1])
    arrived(("pair", 7), precv.at[7])
    for up_e, down_e in zip(DOWN + UP, UP + DOWN):
        hop(3, 0, up_e)
        hop(3, 1, down_e)

    def gather_step(h):
        for e in PARTS:
            gather_x(h, 0, e)
            gather_x(h, 1, e)
        gather_core(h, 0)
        gather_core(h, 1)

    gather_step(1)

    arrived(("pair", 0), precv.at[0])

    def z_total(e):
        total = own[0, e] + precv[0, e].astype(F32)
        for direction in (0, 1):
            arrived(("ring", direction, 3, e), rrecv.at[direction, 3, e])
            total = total + rrecv[direction, 3, e].astype(F32)
        return total

    place = yh * NY + y
    ysums = []
    for both in (LATE[:2], LATE[2:]):
        sums = [z_total(e) for e in both]
        columns = project(
            jnp.concatenate([t[:32] for t in sums], axis=0), jnp.concatenate([t[32:] for t in sums], axis=0)
        ).astype(BF16)
        for i, e in enumerate(both):
            csend[e] = columns[32 * i:32 * i + 32]
            send(("across", e), csend.at[e], crecv.at[place], across(e))
            if e > 0:
                send(("along", e), csend.at[e], crecv.at[place], at_y(e))
            else:
                crecv[place] = columns[32 * i:32 * i + 32]
        ysums += zip(both, sums)
    for e, total in ysums[:3]:
        ysend[e] = total.astype(BF16)
        send(("y", e), ysend.at[e], yrecv.at[e], at_y(e))
    grad = ysums[3][1]

    gather_step(2)

    scale = float(GROUP_TOK) ** -0.5
    arrived(("old",), cmom.at[0])
    for e in LATE[:3]:
        arrived(("along", e), crecv.at[0])
    for e in LATE:
        arrived(("across", e), crecv.at[0])
    shared = crecv[0].astype(F32)
    for i in range(1, NYH * NY):
        shared = shared + crecv[i].astype(F32)
    c2r[x] = (shared * scale + (cmom[0] + cmom[1])).astype(BF16)
    for d in (4, 3, 5, 2, 6, 1, 7):
        send(("rep", d), c2r.at[x], c2r.at[x], at_x(d))

    gather_step(3)

    for e in LATE[:3]:
        arrived(("y", e), yrecv.at[e])
        grad = grad + yrecv[e].astype(F32)
    moment = decayed + grad * scale
    compact = project(moment[:32], moment[32:])
    nm[0, :32] = moment[:32] - lax.dot_general(
        compact, basis0, (((1,), (1,)), ((), ())), precision=HI, preferred_element_type=F32
    )
    nm[0, 32:] = moment[32:] - lax.dot_general(
        compact, basis1, (((1,), (1,)), ((), ())), precision=HI, preferred_element_type=F32
    )
    store(6, nm, nm_hbm)

    for c in started[:-15]:
        c.wait_send()
    del started[:-15]

    far = lax.rem(x + 4, NX)
    for direction in (0, 1):
        for e in LAST[direction]:
            arrived(("gx", direction, 3, e), x_part(far, e))
    send(("gc", 0, 4), x_all(far), x_all(far), sibling)
    for key in [("gc", 0, h) for h in range(5)] + [("gc", 1, h) for h in range(1, 4)]:
        arrived(key, x_all(x))

    for i in range(8):
        w = jnp.concatenate(
            [wf[k, 4 * i:4 * i + 4].reshape(512, 128) for k in range(2)], axis=1
        )
        ig[:, 512 * i:512 * i + 512] = lax.dot_general(
            cot[...], w, (((1,), (1,)), ((), ())), preferred_element_type=F32
        ).astype(BF16)
        if i % 2 == 1:
            done = pl.ds(512 * (i - 1), 1024)
            store(10 + i // 2, ig.at[:, done], ig_hbm.at[:, done])

    for d in range(1, NX):
        arrived(("rep", d), c2r.at[0])
    total = c2r[0].astype(F32)
    for i in range(1, NX):
        total = total + c2r[i].astype(F32)
    total = total * (1.0 / (NX * NYH))
    for i, basis in enumerate((basis0, basis1)):
        rows = slice(32 * i, 32 * i + 32)
        update = lax.dot_general(total, basis, (((1,), (1,)), ((), ())), precision=HI, preferred_element_type=F32)
        up[rows] = update
        nw[rows] = weight[rows] - LEARN_RATE * update

    store(8, up, up_hbm)
    store(9, nw, nw_hbm)
    for c in started:
        c.wait_send()
    for c in stores:
        c.wait()


def finish(ig, nm, up, nw, ig_out, nm_out, up_out, nw_out, ig_v, nm_v, up_v, nw_v, sems):
    moves = [(nm, nm_v, nm_out), (up, up_v, up_out), (nw, nw_v, nw_out)]
    rows = ig.shape[0] // 4
    moves += [tuple(r.at[rows * i:rows * i + rows] for r in (ig, ig_v, ig_out)) for i in range(4)]
    loads = [pltpu.make_async_copy(src, mid, sems.at[0, i]) for i, (src, mid, _) in enumerate(moves)]
    stores = [pltpu.make_async_copy(mid, dst, sems.at[1, i]) for i, (_, mid, dst) in enumerate(moves)]
    for c in loads:
        c.start()
    for load, store in zip(loads, stores):
        load.wait()
        store.start()
    for c in stores:
        c.wait()


def on_device(tokens, cotangent, weight, momentum, column_order):
    hbm = pl.BlockSpec(memory_space=pltpu.HBM)
    shapes = (
        jax.ShapeDtypeStruct(tokens.shape, BF16),
        jax.ShapeDtypeStruct(momentum.shape, F32),
        jax.ShapeDtypeStruct(weight.shape, F32),
        jax.ShapeDtypeStruct(weight.shape, F32),
    )
    table = jnp.asarray(dct_rows())
    results = pl.pallas_call(
        body,
        out_shape=shapes,
        in_specs=[hbm] * 6,
        out_specs=(hbm,) * 4,
        scratch_shapes=[pltpu.VMEM(a.shape, a.dtype) for a in shapes] + [
            pltpu.SMEM(column_order.shape, jnp.int32),
            pltpu.VMEM(tokens.shape, BF16),
            pltpu.VMEM(cotangent.shape, BF16),
            pltpu.VMEM(weight.shape, F32),
            pltpu.VMEM(momentum.shape, F32),
            pltpu.VMEM(table.shape, F32),
            pltpu.VMEM((2, NY * NZ, 2, 4, 16, 128), BF16),
            pltpu.VMEM((NZ, NY, 64, KW), F32),
            pltpu.VMEM((NZ, NY, 64, KW), BF16),
            pltpu.VMEM((NZ, NY, 64, KW), BF16),
            pltpu.VMEM((2, 4, NY, 64, KW), BF16),
            pltpu.VMEM((2, 4, NY, 64, KW), BF16),
            pltpu.VMEM((NY, 64, KW), BF16),
            pltpu.VMEM((NY, 64, KW), BF16),
            pltpu.VMEM((NY, 32, 128), BF16),
            pltpu.VMEM((NYH * NY, 32, 128), BF16),
            pltpu.VMEM((NYH, 32, 128), F32),
            pltpu.VMEM((NX, 32, 128), BF16),
            pltpu.SemaphoreType.DMA((N_SLOTS,)),
            pltpu.SemaphoreType.DMA((N_SLOTS,)),
            pltpu.SemaphoreType.DMA((14,)),
        ],
        compiler_params=pltpu.CompilerParams(
            collective_id=0, has_side_effects=True, vmem_limit_bytes=57 * 1024 * 1024
        ),
        name="demo_step",
    )(column_order, tokens, cotangent, weight, momentum, table)
    return pl.pallas_call(
        finish,
        out_shape=shapes,
        in_specs=[hbm] * 4,
        out_specs=(hbm,) * 4,
        scratch_shapes=[pltpu.VMEM(a.shape, a.dtype) for a in shapes] + [pltpu.SemaphoreType.DMA((2, 7))],
        compiler_params=pltpu.CompilerParams(vmem_limit_bytes=57 * 1024 * 1024),
        name="store_results",
    )(*results)


def solution(mesh):
    in_specs = (
        P(("rep", "fsdp"), None),
        P(("rep", "fsdp"), None),
        P("fsdp", None),
        P("rep", "fsdp", None),
        P(),
    )
    out_specs = (P(("rep", "fsdp"), None), P("rep", "fsdp", None), P("fsdp", None), P("fsdp", None))
    return jax.shard_map(
        on_device, mesh=mesh, in_specs=in_specs, out_specs=out_specs, check_vma=False
    )
```

```python
import math

import jax
import jax.numpy as jnp
import numpy as np
from jax import lax
from jax.experimental import pallas as pl
from jax.experimental.pallas import tpu as pltpu
from jax.sharding import PartitionSpec as P

KW = 256
BLOCK = 64
SEL = 16
NX, NYH, NY, NZ = 8, 2, 4, 8
GROUP_TOK = 12288
MOMENTUM_DECAY = 0.9
LEARN_RATE = 0.05
MESH = pl.DeviceIdType.MESH
F32 = jnp.float32
BF16 = jnp.bfloat16
HI = lax.Precision.HIGHEST

UP = (2, 1)
DOWN = (3, 0)
LATE = (2, 3, 1, 0)

PARTS = (0, 1, 3, 2)
LAST = ((0, 3), (1, 2))


def dct_rows():
    n = np.arange(BLOCK, dtype=np.float64)
    table = np.cos(math.pi * (2.0 * n[None, :] + 1.0) * n[:, None] / (2.0 * BLOCK)) * math.sqrt(2.0 / BLOCK)
    table[0] *= math.sqrt(0.5)
    return np.tile(table.T, (KW // BLOCK, 1)).astype(np.float32)


def make_slots():
    slots = {}

    def slot(*key):
        if key not in slots:
            slots[key] = len(slots)
        return slots[key]

    return slot


N_SLOTS = 128


def body(
    order_hbm, tok_hbm, cot_hbm, weight_hbm, mom_hbm, dct_hbm,
    ig_hbm, nm_hbm, up_hbm, nw_hbm,
    ig, nm, up, nw,
    order, tok, cot, weight, mom, dct,
    wf, own, psend, precv, rsend, rrecv, ysend, yrecv, csend, crecv, cmom, c2r,
    ss, rs, ls,
):
    slot = make_slots()
    local = [
        pltpu.make_async_copy(src, dst, ls.at[i])
        for i, (src, dst) in enumerate((
            (weight_hbm, weight), (cot_hbm, cot), (tok_hbm, tok), (mom_hbm, mom), (dct_hbm, dct), (order_hbm, order),
        ))
    ]
    for c in local:
        c.start()
    rep = lax.axis_index("rep")
    mem = lax.axis_index("fsdp")
    x, yh = rep // 2, rep % 2
    y, z, core = mem // 16, (mem // 2) % 8, mem % 2

    def dev(x_, yh_, y_, z_, core_):
        return (x_ * 2 + yh_, y_ * 16 + z_ * 2 + core_)

    def at_z(d):
        return dev(x, yh, y, lax.rem(z + d, NZ), core)

    def at_y(e):
        return dev(x, yh, lax.rem(y + e, NY), z, core)

    def across(e):
        return dev(x, 1 - yh, lax.rem(y + e, NY), z, core)

    def at_ring_y(d):
        full = lax.rem(yh * NY + y + d, NY * NYH)
        return dev(x, full // NY, full % NY, z, core)

    def at_x(d):
        return dev(lax.rem(x + d, NX), yh, y, z, core)

    sibling = dev(x, yh, y, z, 1 - core)

    partners = [sibling, across(0)]
    partners += [at_z(d) for d in range(1, NZ)]
    partners += [at_x(d) for d in range(1, NX)]
    partners += [at_y(e) for e in range(1, NY)]
    partners += [at_ring_y(d) for d in (1, 2, 6, 7)]
    partners += [across(e) for e in range(1, NY)]
    barrier = pltpu.get_barrier_semaphore()
    for p in partners:
        pl.semaphore_signal(barrier, inc=1, device_id=p, device_id_type=MESH)

    started = []
    stores = []

    def store(i, src, dst):
        c = pltpu.make_async_copy(src, dst, ls.at[i])
        c.start()
        stores.append(c)

    def copy(key, src, dst, device):
        i = slot(*key)
        return pltpu.make_async_remote_copy(
            src_ref=src, dst_ref=dst, send_sem=ss.at[i], recv_sem=rs.at[i],
            device_id=device, device_id_type=MESH,
        )

    def send(key, src, dst, device):
        c = copy(key, src, dst, device)
        c.start()
        started.append(c)

    def arrived(key, dst):
        copy(key, dst, dst, sibling).wait_recv()

    def partial(d):
        for e in range(NY):
            target = lax.rem(y + e, NY) * NZ + lax.rem(z + d, NZ)
            both = lax.dot_general(
                tok[:, pl.ds(pl.multiple_of(target * 128, 128), 128)], cot[...],
                (((0,), (0,)), ((), ())), preferred_element_type=F32,
            )
            low, high = both[:64], both[64:]
            own[d, e] = jnp.where(core == 0, low, high)
            psend[d, e] = jnp.where(core == 0, high, low).astype(BF16)

    def pair(d):
        send(("pair", d), psend.at[d], precv.at[d], sibling)

    chip = y * NZ + z

    def piece(x_):
        return x_ % 2, x_ // 2

    half, rb = piece(x)
    local[0].wait()
    wf[half, chip, core, rb] = weight[
        pl.ds(pl.multiple_of(rb * 16, 16), 16), pl.ds(pl.multiple_of(half * 128, 128), 128)
    ].astype(BF16)
    own_piece = wf.at[half, chip, core, rb]

    pl.semaphore_wait(barrier, len(partners))

    for d in (4, 3, 5, 2, 6, 1, 7):
        send(("gz", d), own_piece, own_piece, at_z(d))

    local[1].wait()
    local[2].wait()
    for d in (4, 3, 5):
        partial(d)
        pair(d)

    def hop(h, direction, e):
        d = 4 - h if direction == 0 else 4 + h
        total = own[d, e] + precv[d, e].astype(F32)
        first = UP if direction == 0 else DOWN
        if h > 1 or (h == 1 and e in first):
            arrived(("ring", direction, h - 1, e), rrecv.at[direction, h - 1, e])
            total = total + rrecv[direction, h - 1, e].astype(F32)
        rsend[direction, h, e] = total.astype(BF16)
        send(
            ("ring", direction, h, e), rsend.at[direction, h, e], rrecv.at[direction, h, e],
            at_z(1 if direction == 0 else 7),
        )

    def x_part(x_, e):
        h_, r_ = piece(x_)
        return wf.at[h_, pl.ds(lax.rem(y + e, NY) * NZ, NZ), core, r_]

    def x_all(x_):
        h_, r_ = piece(x_)
        return wf.at[h_, :, core, r_]

    def origin(h, direction):
        return lax.rem(x + (NX - h if direction == 0 else h), NX)

    def gather_out(e):
        ref = x_part(x, e)
        for step in (2, 1):
            for direction in (0, 1):
                send(("gx", direction, step, e), ref, ref, at_x(step if direction == 0 else NX - step))

    def gather_on(direction, e):
        ref = x_part(origin(2, direction), e)
        arrived(("gx", direction, 2, e), ref)
        for step in (2, 1) if e in LAST[direction] else (1,):
            send(("gx", direction, 2 + step, e), ref, ref, at_x(step if direction == 0 else NX - step))

    def gather_end(h, direction):
        for e in PARTS:
            arrived(("gx", direction, h, e), x_part(origin(h, direction), e))
        gather_core(h, direction)

    def gather_core(h, direction):
        ref = x_all(origin(h, direction))
        send(("gc", direction, h), ref, ref, sibling)

    for d in (2, 6):
        partial(d)
        pair(d)
    arrived(("pair", 4), precv.at[4])
    for i in range(2):
        hop(0, 0, UP[i])
        hop(0, 1, DOWN[i])
    for d in (1, 7, 0):
        partial(d)
        pair(d)
    arrived(("pair", 3), precv.at[3])
    arrived(("pair", 5), precv.at[5])
    for i in range(2):
        hop(1, 0, DOWN[i])
        hop(1, 1, UP[i])

    for i in range(2):
        hop(1, 0, UP[i])
        hop(1, 1, DOWN[i])

    for d in range(1, NZ):
        arrived(("gz", d), own_piece)
    y_block = x_part(x, 0)
    for d in (1, 7, 2):
        send(("gy", d), y_block, y_block, at_ring_y(d))
    gather_out(0)

    for i in (3, 4, 5):
        local[i].wait()

    row = lax.broadcasted_iota(jnp.int32, (BLOCK, 128), 0)
    lane = lax.broadcasted_iota(jnp.int32, (BLOCK, 128), 1)
    picked = jnp.zeros((BLOCK, 128), F32)
    for s in range(SEL):
        picked = jnp.where((lane % SEL == s) & (row == order[s]), 1.0, picked)
    wide = lax.dot_general(dct[...], picked, (((1,), (0,)), ((), ())), precision=HI, preferred_element_type=F32)
    row_block = lax.broadcasted_iota(jnp.int32, (KW, 128), 0) // BLOCK
    lane_block = lax.broadcasted_iota(jnp.int32, (KW, 128), 1) // SEL
    basis0 = jnp.where(row_block == lane_block, wide, 0.0)
    basis1 = jnp.where(row_block + 4 == lane_block, wide, 0.0)

    def project(upper, lower):
        return lax.dot_general(
            upper, basis0, (((1,), (0,)), ((), ())), precision=HI, preferred_element_type=F32
        ) + lax.dot_general(
            lower, basis1, (((1,), (0,)), ((), ())), precision=HI, preferred_element_type=F32
        )

    decayed = MOMENTUM_DECAY * mom[0]
    cmom[yh] = project(decayed[:32], decayed[32:])
    send(("old",), cmom.at[yh], cmom.at[yh], across(0))

    arrived(("pair", 2), precv.at[2])
    arrived(("pair", 6), precv.at[6])
    for up_e, down_e in zip(DOWN + UP, UP + DOWN):
        hop(2, 0, up_e)
        hop(2, 1, down_e)

    for d, e in ((7, 1), (1, 3), (2, 2)):
        arrived(("gy", d), x_part(x, e))
        gather_out(e)
    gather_core(0, 0)

    arrived(("pair", 1), precv.at[1])
    arrived(("pair", 7), precv.at[7])
    for up_e, down_e in zip(DOWN + UP, UP + DOWN):
        hop(3, 0, up_e)
        hop(3, 1, down_e)

    for e in PARTS:
        gather_on(0, e)
        gather_on(1, e)
    gather_core(2, 0)
    gather_core(2, 1)

    arrived(("pair", 0), precv.at[0])

    def z_total(e):
        total = own[0, e] + precv[0, e].astype(F32)
        for direction in (0, 1):
            arrived(("ring", direction, 3, e), rrecv.at[direction, 3, e])
            total = total + rrecv[direction, 3, e].astype(F32)
        return total

    place = yh * NY + y
    ysums = []
    for both in (LATE[:2], LATE[2:]):
        sums = [z_total(e) for e in both]
        columns = project(
            jnp.concatenate([t[:32] for t in sums], axis=0), jnp.concatenate([t[32:] for t in sums], axis=0)
        ).astype(BF16)
        for i, e in enumerate(both):
            csend[e] = columns[32 * i:32 * i + 32]
            send(("across", e), csend.at[e], crecv.at[place], across(e))
            if e > 0:
                send(("along", e), csend.at[e], crecv.at[place], at_y(e))
            else:
                crecv[place] = columns[32 * i:32 * i + 32]
        ysums += zip(both, sums)
    for e, total in ysums[:3]:
        ysend[e] = total.astype(BF16)
        send(("y", e), ysend.at[e], yrecv.at[e], at_y(e))
    grad = ysums[3][1]

    gather_end(1, 0)
    gather_end(1, 1)

    scale = float(GROUP_TOK) ** -0.5
    arrived(("old",), cmom.at[0])
    for e in LATE[:3]:
        arrived(("along", e), crecv.at[0])
    for e in LATE:
        arrived(("across", e), crecv.at[0])
    shared = crecv[0].astype(F32)
    for i in range(1, NYH * NY):
        shared = shared + crecv[i].astype(F32)
    c2r[x] = (shared * scale + (cmom[0] + cmom[1])).astype(BF16)
    for d in (4, 3, 5, 2, 6, 1, 7):
        send(("rep", d), c2r.at[x], c2r.at[x], at_x(d))

    gather_end(3, 0)
    gather_end(3, 1)

    far = lax.rem(x + 4, NX)
    for direction in (0, 1):
        for e in LAST[direction]:
            arrived(("gx", direction, 4, e), x_part(far, e))
    send(("gc", 0, 4), x_all(far), x_all(far), sibling)
    for e in LATE[:3]:
        arrived(("y", e), yrecv.at[e])
        grad = grad + yrecv[e].astype(F32)
    moment = decayed + grad * scale
    compact = project(moment[:32], moment[32:])
    nm[0, :32] = moment[:32] - lax.dot_general(
        compact, basis0, (((1,), (1,)), ((), ())), precision=HI, preferred_element_type=F32
    )
    nm[0, 32:] = moment[32:] - lax.dot_general(
        compact, basis1, (((1,), (1,)), ((), ())), precision=HI, preferred_element_type=F32
    )
    store(6, nm, nm_hbm)

    for c in started[:-15]:
        c.wait_send()
    del started[:-15]

    for key in [("gc", 0, h) for h in range(5)] + [("gc", 1, h) for h in range(1, 4)]:
        arrived(key, x_all(x))

    for i in range(8):
        w = jnp.concatenate(
            [wf[k, 4 * i:4 * i + 4].reshape(512, 128) for k in range(2)], axis=1
        )
        ig[:, 512 * i:512 * i + 512] = lax.dot_general(
            cot[...], w, (((1,), (1,)), ((), ())), preferred_element_type=F32
        ).astype(BF16)
        if i % 2 == 1:
            done = pl.ds(512 * (i - 1), 1024)
            store(10 + i // 2, ig.at[:, done], ig_hbm.at[:, done])

    for d in range(1, NX):
        arrived(("rep", d), c2r.at[0])
    total = c2r[0].astype(F32)
    for i in range(1, NX):
        total = total + c2r[i].astype(F32)
    total = total * (1.0 / (NX * NYH))
    for i, basis in enumerate((basis0, basis1)):
        rows = slice(32 * i, 32 * i + 32)
        update = lax.dot_general(total, basis, (((1,), (1,)), ((), ())), precision=HI, preferred_element_type=F32)
        up[rows] = update
        nw[rows] = weight[rows] - LEARN_RATE * update

    store(8, up, up_hbm)
    store(9, nw, nw_hbm)
    for c in started:
        c.wait_send()
    for c in stores:
        c.wait()


def finish(ig, nm, up, nw, ig_out, nm_out, up_out, nw_out, ig_v, nm_v, up_v, nw_v, sems):
    rows = ig.shape[0] // 4
    moves = [tuple(r.at[rows * i:rows * i + rows] for r in (ig, ig_v, ig_out)) for i in range(4)]
    moves += [(nm, nm_v, nm_out), (up, up_v, up_out), (nw, nw_v, nw_out)]
    loads = [pltpu.make_async_copy(src, mid, sems.at[0, i]) for i, (src, mid, _) in enumerate(moves)]
    stores = [pltpu.make_async_copy(mid, dst, sems.at[1, i]) for i, (_, mid, dst) in enumerate(moves)]
    for c in loads:
        c.start()
    for load, store in zip(loads, stores):
        load.wait()
        store.start()
    for c in stores:
        c.wait()


def on_device(tokens, cotangent, weight, momentum, column_order):
    hbm = pl.BlockSpec(memory_space=pltpu.HBM)
    shapes = (
        jax.ShapeDtypeStruct(tokens.shape, BF16),
        jax.ShapeDtypeStruct(momentum.shape, F32),
        jax.ShapeDtypeStruct(weight.shape, F32),
        jax.ShapeDtypeStruct(weight.shape, F32),
    )
    table = jnp.asarray(dct_rows())
    results = pl.pallas_call(
        body,
        out_shape=shapes,
        in_specs=[hbm] * 6,
        out_specs=(hbm,) * 4,
        scratch_shapes=[pltpu.VMEM(a.shape, a.dtype) for a in shapes] + [
            pltpu.SMEM(column_order.shape, jnp.int32),
            pltpu.VMEM(tokens.shape, BF16),
            pltpu.VMEM(cotangent.shape, BF16),
            pltpu.VMEM(weight.shape, F32),
            pltpu.VMEM(momentum.shape, F32),
            pltpu.VMEM(table.shape, F32),
            pltpu.VMEM((2, NY * NZ, 2, 4, 16, 128), BF16),
            pltpu.VMEM((NZ, NY, 64, KW), F32),
            pltpu.VMEM((NZ, NY, 64, KW), BF16),
            pltpu.VMEM((NZ, NY, 64, KW), BF16),
            pltpu.VMEM((2, 4, NY, 64, KW), BF16),
            pltpu.VMEM((2, 4, NY, 64, KW), BF16),
            pltpu.VMEM((NY, 64, KW), BF16),
            pltpu.VMEM((NY, 64, KW), BF16),
            pltpu.VMEM((NY, 32, 128), BF16),
            pltpu.VMEM((NYH * NY, 32, 128), BF16),
            pltpu.VMEM((NYH, 32, 128), F32),
            pltpu.VMEM((NX, 32, 128), BF16),
            pltpu.SemaphoreType.DMA((N_SLOTS,)),
            pltpu.SemaphoreType.DMA((N_SLOTS,)),
            pltpu.SemaphoreType.DMA((14,)),
        ],
        compiler_params=pltpu.CompilerParams(
            collective_id=0, has_side_effects=True, vmem_limit_bytes=57 * 1024 * 1024
        ),
        name="demo_step",
    )(column_order, tokens, cotangent, weight, momentum, table)
    return pl.pallas_call(
        finish,
        out_shape=shapes,
        in_specs=[hbm] * 4,
        out_specs=(hbm,) * 4,
        scratch_shapes=[pltpu.VMEM(a.shape, a.dtype) for a in shapes] + [pltpu.SemaphoreType.DMA((2, 7))],
        compiler_params=pltpu.CompilerParams(vmem_limit_bytes=57 * 1024 * 1024),
        name="store_results",
    )(*results)


def solution(mesh):
    in_specs = (
        P(("rep", "fsdp"), None),
        P(("rep", "fsdp"), None),
        P("fsdp", None),
        P("rep", "fsdp", None),
        P(),
    )
    out_specs = (P(("rep", "fsdp"), None), P("rep", "fsdp", None), P("fsdp", None), P("fsdp", None))
    return jax.shard_map(
        on_device, mesh=mesh, in_specs=in_specs, out_specs=out_specs, check_vma=False
    )
```
